32 devices in a mesh: groups: 2 (over x), tp: 16 (over z, y, core).
Axes of the slice: x: 2, y: 2, z: 4, core: 2. Of those that a mesh axis runs over, the one named last changes fastest.
Arguments:
- hidden: bfloat16 [1536, 28672], P('groups', 'tp'), parts along dimension 0, may hold values from -6 to 6
- positions: int32 [768], P('groups'), parts along dimension 0, may hold values from 0 to 767, as said below
- adapter_rows: int32 [28672], P('tp'), may hold values from 0 to 28671, as said below
- adapter_a: bfloat16 [28672, 64], P('tp'), may hold values from -1 to 1
- adapter_b: bfloat16 [64, 8192], P(None, 'tp'), may hold values from -0.03125 to 0.03125
- frozen_down_weight: bfloat16 [28672, 8192], P('tp'), may hold values from -0.03125 to 0.03125
- residual: bfloat16 [768, 8192], P(('groups', 'tp')), parts along dimension 0, may hold values from -6 to 6
- gain: bfloat16 [8192], replicated, may hold values from 0.099609375 to 1.8984375
Outputs:
- normed: bfloat16 [768, 8192], P('groups'), parts along dimension 0
The draws below stay inside these ranges and needn't reach their ends.
There are 2 independent parts, one for each index of `groups`. The reference program is written for one: setup_inputs(seed, part) draws one part's arguments, and reference() takes and returns one part's arrays. A program takes and returns all parts, laid end to end along the dimension named above; an argument that names none is the same for every part. Nothing has to cross between parts.
Inputs may be any that keep to these rules, and one draw needn't show every extreme that they name: `adapter_rows`: A permutation of the row numbers. Of the 1792 entries in each aligned block of 1792 positions, at most 224 lie in any one aligned block of 1792 row numbers, and every block of positions has exactly 224 in one block of row numbers. `positions`: Distinct.
All inputs are finite; a program needn't handle non-finite values.
Results may differ from the reference program's by a relative error of at most 0.013.
Values may be sent and summed in bfloat16 or wider, within the bound.
A program may use at most 128 MiB of HBM per device.

```python
import jax
import jax.numpy as jnp
from jax import lax

D = 8192
FF = 28672
R = 64
TOKENS = 384
BUF = 768
ROWS_TP = 1792
N_TP = 16


def draw_positions(key, part):
    key = jax.random.fold_in(key, 11)
    return jax.random.permutation(key, BUF)[:TOKENS].astype(jnp.int32)


def draw_adapter_rows(key, part):
    key = jax.random.fold_in(key, 23)
    key_owner, key_order, key_shuffle = jax.random.split(key, 3)
    own_rows = FF // N_TP
    share = own_rows // N_TP
    sigma = jax.random.permutation(key_owner, N_TP).astype(jnp.int32)
    sigma_next = jnp.roll(sigma, -1)
    owner_grid = jnp.arange(N_TP, dtype=jnp.int32)[None, :]
    counts = share + share * (owner_grid == sigma[:, None]).astype(jnp.int32) - share * (owner_grid == sigma_next[:, None]).astype(jnp.int32)
    starts = jnp.cumsum(counts, axis=0) - counts
    ends = starts + counts
    offsets = jnp.cumsum(counts, axis=1) - counts
    order = jax.vmap(lambda k: jax.random.permutation(k, own_rows))(jax.random.split(key_order, N_TP)).astype(jnp.int32)
    position = jnp.arange(own_rows, dtype=jnp.int32)
    source = jnp.sum((ends.T[:, None, :] <= position[None, :, None]).astype(jnp.int32), axis=2)
    begin = jnp.take_along_axis(starts.T, source, axis=1)
    skipped = jnp.take_along_axis(offsets.T, source, axis=1)
    slot_index = source * own_rows + skipped + position[None, :] - begin
    values = jnp.arange(N_TP, dtype=jnp.int32)[:, None] * own_rows + order
    table = jnp.zeros((FF,), jnp.int32).at[slot_index.reshape(-1)].set(values.reshape(-1))
    shuffle = jax.vmap(lambda k: jax.random.permutation(k, own_rows))(jax.random.split(key_shuffle, N_TP)).astype(jnp.int32)
    picks = jnp.arange(N_TP, dtype=jnp.int32)[:, None] * own_rows + shuffle
    return jnp.take(table, picks.reshape(-1)).astype(jnp.int32)


def level_of(stream_key, dims, cuts, low, high):
    loudness, own = 1.0, jax.random.fold_in(stream_key, 6)
    for dim, blocks in cuts:
        draws = jnp.exp(jax.random.uniform(jax.random.fold_in(own, dim), (blocks,), jnp.float32, low / len(cuts), high / len(cuts)))
        loudness = loudness * jnp.repeat(draws, dims[dim] // blocks).reshape([-1 if axis == dim else 1 for axis in range(len(dims))])
    return loudness


def bell_draw(own_key, extent, deviation, limit, pieces=(), held_as=jnp.bfloat16):
    array = jax.random.normal(own_key, extent, jnp.float32) * deviation
    if len(pieces) > 0:
        array = level_of(own_key, extent, pieces, -0.22, 0.18) * array
    return jnp.clip(array, min=-limit, max=limit).astype(held_as)


def setup_inputs(seed: int = 0, part: int = 0) -> dict:
    key_list = jax.random.split(jax.random.key(seed), 9)
    own_keys = jax.random.split(jax.random.fold_in(key_list[8], part), 9)
    hidden = bell_draw(own_keys[0], (BUF, FF), 1.0, 6.0, ((1, 16),))
    positions = draw_positions(jax.random.fold_in(jax.random.fold_in(key_list[8], part), 71), part)
    adapter_rows = draw_adapter_rows(jax.random.fold_in(key_list[8], 71), part)
    adapter_a = bell_draw(key_list[3], (FF, R), 0.0625, 1.0, ((0, 16),))
    adapter_b = bell_draw(key_list[4], (R, D), FF ** -0.5, 0.03125, ((1, 16),))
    frozen_down_weight = bell_draw(key_list[5], (FF, D), FF ** -0.5, 0.03125, ((0, 16),))
    residual = bell_draw(own_keys[6], (TOKENS, D), 1.0, 6.0, ((0, 16),))
    gain = jnp.clip(1.0 + 0.18 * jax.random.normal(key_list[7], (D,), jnp.float32), 0.099609375, 1.8984375).astype(jnp.bfloat16)
    return {"hidden": hidden, "positions": positions, "adapter_rows": adapter_rows, "adapter_a": adapter_a, "adapter_b": adapter_b, "frozen_down_weight": frozen_down_weight, "residual": residual, "gain": gain}


adapter_scale = 2.0
norm_eps = 1e-05

def reference(hidden, positions, adapter_rows, adapter_a, adapter_b, frozen_down_weight, residual, gain):
    factor_a = jnp.zeros((FF, R), adapter_a.dtype).at[adapter_rows].set(adapter_a)
    late_rows = jnp.take(hidden, positions, axis=0)

    def update_block(running, block_index):
        row_start = block_index * ROWS_TP
        frozen_block = lax.dynamic_slice_in_dim(frozen_down_weight, row_start, ROWS_TP, 0)
        a_block = lax.dynamic_slice_in_dim(factor_a, row_start, ROWS_TP, 0)
        low_rank_update = jnp.dot(a_block, adapter_b, preferred_element_type=jnp.float32)
        merged_weight = (frozen_block.astype(jnp.float32) + adapter_scale * low_rank_update).astype(frozen_down_weight.dtype)
        trailing_columns = lax.dynamic_slice_in_dim(late_rows, row_start, ROWS_TP, 1)
        block_sum = jnp.dot(trailing_columns, merged_weight, preferred_element_type=jnp.float32).astype(jnp.bfloat16)
        block_sum = lax.optimization_barrier(block_sum)
        return (running + block_sum.astype(jnp.float32), None)
    running, _ = lax.scan(update_block, jnp.zeros((TOKENS, D), jnp.float32), jnp.arange(N_TP, dtype=jnp.int32))
    stream = residual.astype(jnp.float32) + running
    inverse_rms = lax.rsqrt(lax.optimization_barrier(jnp.mean(stream * stream, axis=-1, keepdims=True)) + norm_eps)
    return (stream * inverse_rms * gain.astype(jnp.float32)).astype(jnp.bfloat16)
```

```python
import functools

import jax
import jax.numpy as jnp
from jax import lax
from jax.experimental import pallas as pl
from jax.experimental.pallas import tpu as pltpu
from jax.sharding import PartitionSpec as P

adapter_scale = 2.0
norm_eps = 1e-05
CHUNKS = 8
PIECES = 4
W_SLOTS = 3
BF16 = jnp.bfloat16
F32 = jnp.float32
NT = (((1,), (1,)), ((), ()))


def kernel(
    cfg,
    pos_ref, hidden_ref, ids_ref, aa_ref, b_ref, w_hbm, res_ref, gain_ref,
    out_hbm,
    wbuf, late, code, idrows, abuf, got, uacc, tsend, trecv, bfull,
    pbuf, c_send, c_recv, y_send, y_recv, y_own, z_send, z_recv, stream, nbuf,
    w_sem, cs, cr, ys, yr, zs, zr, as_, ar, ts, tr,
    bzs, bzr, bys, byr, bcs, bcr, gzs, gzr, gys, gyr, gcs, gcr, loc,
):
    tp, nz, rows, tokens, half, hp, own_rows, d_model = cfg
    n = CHUNKS
    hd = d_model // 2
    cw = hd // n
    me = lax.axis_index("tp")
    z, y, c = me // 4, (me // 2) % 2, me % 2
    sib = me + 1 - 2 * c
    ypeer = me + 2 - 4 * y
    nb = 2 * nz

    def remote(src, dst, send, recv, dev):
        return pltpu.make_async_remote_copy(
            src_ref=src, dst_ref=dst, send_sem=send, recv_sem=recv,
            device_id={"tp": dev}, device_id_type=pl.DeviceIdType.MESH,
        )

    def w_copies(j):
        slot = lax.rem(j, W_SLOTS)
        return [
            pltpu.make_async_copy(
                w_hbm.at[:, pl.ds(pl.multiple_of(h * hd + j * cw, 128), cw)],
                wbuf.at[slot, :, pl.ds(h * cw, cw)],
                w_sem.at[slot, h],
            )
            for h in range(2)
        ]

    for j in range(W_SLOTS - 1):
        for copy in w_copies(j):
            copy.start()

    barrier = pltpu.get_barrier_semaphore()

    @pl.loop(1, tp)
    def _(i):
        pl.semaphore_signal(
            barrier, inc=1, device_id={"tp": lax.rem(me + i, tp)},
            device_id_type=pl.DeviceIdType.MESH,
        )

    buf_rows = hidden_ref.shape[0]
    pick = jnp.where(
        pos_ref[...] == lax.broadcasted_iota(jnp.int32, (tokens, buf_rows), 1), 1.0, 0.0
    ).astype(BF16)
    lw = 256 if own_rows % 256 == 0 else 128
    for t in range(own_rows // lw):
        late[:, t * lw : (t + 1) * lw] = jnp.dot(
            pick, hidden_ref[:, t * lw : (t + 1) * lw], preferred_element_type=F32
        ).astype(BF16)

    ids = ids_ref[...]
    first = lax.broadcasted_iota(jnp.int32, (tp, 1), 0) * own_rows
    mine = (ids >= first) & (ids < first + own_rows)
    hot = jnp.where(mine, 1.0, 0.0)
    local = jnp.sum(jnp.where(mine, ids - first, 0), axis=0, keepdims=True)
    before = jnp.where(
        lax.broadcasted_iota(jnp.int32, (128, 128), 0)
        < lax.broadcasted_iota(jnp.int32, (128, 128), 1), 1.0, 0.0,
    ).astype(BF16)
    carry = jnp.zeros((tp, 1), F32)
    base = (lax.broadcasted_iota(jnp.int32, (tp, 1), 0) * 256).astype(F32)
    for t in range(own_rows // 128):
        part = hot[:, t * 128 : (t + 1) * 128]
        rank = jnp.dot(part.astype(BF16), before, preferred_element_type=F32) + carry
        rank = rank + jnp.where(rank >= half, 128.0 - half, 0.0)
        code[:, t * 128 : (t + 1) * 128] = jnp.sum(
            part * (rank + base), axis=0, keepdims=True
        ).astype(jnp.int32)
        carry = carry + jnp.sum(part, axis=1, keepdims=True)
    which = lax.broadcasted_iota(jnp.int32, (16, own_rows), 0)
    idrows[...] = jnp.where(
        which == 0, (local >> 7).astype(F32),
        jnp.where(which == 1, (local & 127).astype(F32), jnp.where(which == 2, 1.0, 0.0)),
    ).astype(BF16)
    uacc[...] = jnp.zeros_like(uacc)

    pl.semaphore_wait(barrier, tp - 1)

    def b_z(i):
        return remote(b_ref, bfull.at[me], bzs.at[i - 1], bzr.at[i - 1], lax.rem(me + 4 * i, tp))

    def b_y(i):
        blk = lax.rem(me + 4 * nz - 4 * i, tp)
        return remote(bfull.at[blk], bfull.at[blk], bys.at[i], byr.at[i], ypeer)

    def b_c(i, other):
        blk = lax.rem(me + 4 * nz - 4 * i, tp)
        if other:
            blk = blk + 2 - 4 * y
        k = i + other * nz
        return remote(bfull.at[blk], bfull.at[blk], bcs.at[k], bcr.at[k], sib)

    bfull[me] = b_ref[...]
    for i in range(1, nz):
        b_z(i).start()
    b_y(0).start()
    b_c(0, 0).start()

    def core_copy(j):
        return remote(c_send.at[j], c_recv.at[j], cs.at[j], cr.at[j], sib)

    def y_copy(j):
        return remote(y_send.at[j], y_recv.at[j], ys.at[j], yr.at[j], ypeer)

    def z_copy(j, i):
        to = lax.rem(z + i, nz)
        return remote(
            z_send.at[j, to], z_recv.at[j, i - 1], zs.at[j, i - 1], zr.at[j, i - 1],
            lax.rem(me + 4 * i, tp),
        )

    def a_copy(i):
        to = lax.rem(me + i, tp)
        return remote(abuf.at[to], got.at[i], as_.at[i], ar.at[i], to)

    def t_copy(i):
        to = lax.rem(me + i, tp)
        blk = (to % 2) * nb + ((to // 2) % 2) * nz + to // 4
        return remote(tsend.at[blk], trecv.at[i], ts.at[i], tr.at[i], to)

    lane = lax.broadcasted_iota(jnp.int32, (hp, 128), 1)
    per = 2 * tp // n

    def send_rows(i):
        to = lax.rem(me + i, tp)
        spot = jnp.where(
            code[...] == to * 256 + lax.broadcasted_iota(jnp.int32, (256, own_rows), 0), 1.0, 0.0
        ).astype(BF16)
        picked = jnp.dot(spot, aa_ref[...], preferred_element_type=F32)
        rows_out = jnp.where(lane < 64, picked[:hp], picked[128 : 128 + hp])
        marks = lax.dot_general(idrows[...], spot, NT, preferred_element_type=F32)
        block = jnp.concatenate([rows_out, marks[:8, :128], marks[:8, 128:]], axis=0).astype(BF16)

        @pl.when(i > 0)
        def _():
            abuf[to] = block
            a_copy(i).start()

        @pl.when(i == 0)
        def _():
            got[0] = block

    def use_rows(i):
        @pl.when(i > 0)
        def _():
            a_copy(i).wait_recv()

        block = got[i]
        marks = block[hp:].astype(F32)
        found = []
        for h in range(2):
            m = marks[8 * h : 8 * h + 8]
            row = jnp.where(m[2:3] > 0.5, m[0:1] * 128.0 + m[1:2], -1.0).astype(jnp.int32)
            found.append(row)
        row = jnp.concatenate(found, axis=1)
        spot = jnp.where(
            row == lax.broadcasted_iota(jnp.int32, (own_rows, 256), 0), 1.0, 0.0
        ).astype(BF16)
        lq = jnp.dot(late[...], spot, preferred_element_type=F32).astype(BF16)
        k = hp + 16
        for h in range(2):
            uacc[h] += jnp.dot(lq[:, 128 * h : 128 * h + k], block, preferred_element_type=F32)

    @pl.loop(0, n + 5)
    def _(s):
        @pl.when(s < n)
        def _():
            @pl.when(s + W_SLOTS - 1 < n)
            def _():
                for copy in w_copies(s + W_SLOTS - 1):
                    copy.start()

            for copy in w_copies(s):
                copy.wait()
            slot, ps = lax.rem(s, W_SLOTS), lax.rem(s, 2)
            for h in range(2):
                r = jnp.dot(
                    late[...], wbuf[slot, :, h * cw : (h + 1) * cw], preferred_element_type=F32
                )
                pbuf[ps, :, h * rows : (h + 1) * rows, :] = r.reshape(tp, rows, cw)
            c_send[s] = pbuf[ps, pl.ds((1 - c) * nb, nb)].astype(BF16)
            core_copy(s).start()

        @pl.when((s >= 1) & (s < n + 1))
        def _():
            j = s - 1
            ps = lax.rem(j, 2)
            core_copy(j).wait_recv()
            y_send[j] = (
                pbuf[ps, pl.ds(c * nb + (1 - y) * nz, nz)]
                + c_recv[j, pl.ds((1 - y) * nz, nz)].astype(F32)
            ).astype(BF16)
            y_copy(j).start()
            y_own[j] = pbuf[ps, pl.ds(c * nb + y * nz, nz)] + c_recv[
                j, pl.ds(y * nz, nz)
            ].astype(F32)

        @pl.when(s < n // 2)
        def _():
            @pl.loop(0, per)
            def _(k):
                send_rows(s * per + k)

        @pl.when((s >= n // 2) & (s < n))
        def _():
            @pl.loop(0, per)
            def _(k):
                use_rows((s - n // 2) * per + k)

        @pl.when(s == 1)
        def _():
            for i in range(1, nz):
                b_z(i).wait_recv()
                b_y(i).start()
                b_c(i, 0).start()

        @pl.when(s == 3)
        def _():
            for i in range(nz):
                b_y(i).wait_recv()
                b_c(i, 1).start()

        @pl.when(s == n - 1)
        def _():
            low = uacc[0][:, :64] + uacc[1][:, 64:]
            low = jnp.concatenate([low, jnp.zeros_like(low)], axis=1)
            tsend[...] = low.reshape(tp, rows, 128)

            @pl.loop(1, tp)
            def _(i):
                t_copy(i).start()

        @pl.when((s >= 3) & (s < n + 3))
        def _():
            j = s - 3
            y_copy(j).wait_recv()
            total = y_own[j] + y_recv[j].astype(F32)
            z_send[j] = total.astype(BF16)
            for i in range(1, nz):
                z_copy(j, i).start()
            y_own[j] = total

        @pl.when(s >= 5)
        def _():
            j = s - 5
            total = y_own[j, z]
            for i in range(1, nz):
                z_copy(j, i).wait_recv()
                total = total + z_recv[j, i - 1].astype(F32)
            stream[:, pl.ds(pl.multiple_of(j * cw, 128), cw)] = total

    @pl.loop(1, tp)
    def _(i):
        t_copy(i).wait_recv()

    low = tsend[c * nb + y * nz + z]
    for i in range(1, tp):
        low = low + trecv[i]
    low = (low[:, :64] * adapter_scale).astype(BF16)
    for i in range(nz):
        b_c(i, 0).wait_recv()
        b_c(i, 1).wait_recv()
    bw = d_model // tp
    square = jnp.zeros((rows, 1), F32)
    for k in range(tp):
        h, at = (k * bw) // hd, (k * bw) % hd
        v = stream[h * rows : (h + 1) * rows, at : at + bw]
        v = v + res_ref[:, k * bw : (k + 1) * bw].astype(F32)
        v = v + jnp.dot(low, bfull[k], preferred_element_type=F32)
        stream[h * rows : (h + 1) * rows, at : at + bw] = v
        square = square + jnp.sum(v * v, axis=1, keepdims=True)
    inverse = lax.rsqrt(square * (1.0 / d_model) + norm_eps)

    pw = hd // PIECES

    def piece(ref, p):
        return ref.at[:, pl.ds(p * pw, pw)]

    def g_own(p):
        return pltpu.make_async_copy(piece(nbuf, p), piece(out_hbm.at[me], p), loc.at[p])

    def g_z(p, i):
        return remote(
            piece(nbuf, p), piece(out_hbm.at[me], p), gzs.at[p, i - 1], gzr.at[p, i - 1],
            lax.rem(me + 4 * i, tp),
        )

    def g_blk(i):
        return lax.rem(me + 4 * nz - 4 * i, tp)

    def g_y(p, i):
        dst = piece(out_hbm.at[g_blk(i)], p)
        src = piece(nbuf, p) if i == 0 else dst
        return remote(src, dst, gys.at[p, i], gyr.at[p, i], ypeer)

    def g_c(p, i, other):
        blk = g_blk(i) + (2 - 4 * y if other else 0)
        dst = piece(out_hbm.at[blk], p)
        src = piece(nbuf, p) if (i == 0 and not other) else dst
        k = i + other * nz
        return remote(src, dst, gcs.at[p, k], gcr.at[p, k], sib)

    for p in range(PIECES):
        v = []
        for h in range(2):
            v.append(
                stream[h * rows : (h + 1) * rows, p * pw : (p + 1) * pw]
                * inverse
                * gain_ref[h : h + 1, p * pw : (p + 1) * pw]
            )
        nbuf[:, p * pw : (p + 1) * pw] = jnp.concatenate(v, axis=0).astype(BF16)
        g_y(p, 0).start()
        for i in range(1, nz):
            g_z(p, i).start()
        g_c(p, 0, 0).start()
        g_own(p).start()

    items = [(p, i) for p in range(PIECES) for i in range(nz)]
    lag = nz
    for q in range(len(items) + lag):
        if q < len(items):
            p, i = items[q]
            if i > 0:
                g_z(p, i).wait_recv()
                g_y(p, i).start()
                g_c(p, i, 0).start()
        if q >= lag:
            p, i = items[q - lag]
            g_y(p, i).wait_recv()
            g_c(p, i, 1).start()

    for p in range(PIECES):
        g_own(p).wait()
        for i in range(nz):
            g_c(p, i, 0).wait()
            g_c(p, i, 1).wait()
            g_y(p, i).wait_send()
            if i > 0:
                g_z(p, i).wait_send()
    for i in range(nz):
        b_y(i).wait_send()
        b_c(i, 0).wait_send()
        b_c(i, 1).wait_send()
        if i > 0:
            b_z(i).wait_send()

    @pl.loop(1, tp)
    def _(i):
        a_copy(i).wait_send()
        t_copy(i).wait_send()

    @pl.loop(0, n)
    def _(j):
        core_copy(j).wait_send()
        y_copy(j).wait_send()
        for i in range(1, nz):
            z_copy(j, i).wait_send()


def on_device(
    hidden, positions, adapter_rows, adapter_a, adapter_b, frozen_down_weight, residual, gain
):
    tp = lax.axis_size("tp")
    nz = tp // 4
    rows, d_model = residual.shape
    own_rows = frozen_down_weight.shape[0]
    tokens = rows * tp
    half = own_rows // tp
    hp = (half + 15) // 16 * 16
    hd = d_model // 2
    cw = hd // CHUNKS
    order = positions.reshape(nz, 2, 2, rows).transpose(2, 1, 0, 3).reshape(tokens, 1)
    doubled = jnp.concatenate([adapter_a, adapter_a], axis=1)
    n = CHUNKS
    dma = pltpu.SemaphoreType.DMA
    blk = (2 * rows, cw)
    scratch = [
        pltpu.VMEM((W_SLOTS, own_rows, 2 * cw), BF16),
        pltpu.VMEM((tokens, own_rows), BF16),
        pltpu.VMEM((1, own_rows), jnp.int32),
        pltpu.VMEM((16, own_rows), BF16),
        pltpu.VMEM((tp, hp + 16, 128), BF16),
        pltpu.VMEM((tp, hp + 16, 128), BF16),
        pltpu.VMEM((2, tokens, 128), F32),
        pltpu.VMEM((tp, rows, 128), F32),
        pltpu.VMEM((tp, rows, 128), F32),
        pltpu.VMEM((tp,) + adapter_b.shape, BF16),
        pltpu.VMEM((2, tp) + blk, F32),
        pltpu.VMEM((n, 2 * nz) + blk, BF16),
        pltpu.VMEM((n, 2 * nz) + blk, BF16),
        pltpu.VMEM((n, nz) + blk, BF16),
        pltpu.VMEM((n, nz) + blk, BF16),
        pltpu.VMEM((n, nz) + blk, F32),
        pltpu.VMEM((n, nz) + blk, BF16),
        pltpu.VMEM((n, nz - 1) + blk, BF16),
        pltpu.VMEM((2 * rows, hd), F32),
        pltpu.VMEM((2 * rows, hd), BF16),
        dma((W_SLOTS, 2)),
        dma((n,)), dma((n,)),
        dma((n,)), dma((n,)),
        dma((n, nz - 1)), dma((n, nz - 1)),
        dma((tp,)), dma((tp,)),
        dma((tp,)), dma((tp,)),
        dma((nz - 1,)), dma((nz - 1,)),
        dma((nz,)), dma((nz,)),
        dma((2 * nz,)), dma((2 * nz,)),
        dma((PIECES, nz - 1)), dma((PIECES, nz - 1)),
        dma((PIECES, nz)), dma((PIECES, nz)),
        dma((PIECES, 2 * nz)), dma((PIECES, 2 * nz)),
        dma((PIECES,)),
    ]
    vmem = pl.BlockSpec(memory_space=pltpu.VMEM)
    hbm = pl.BlockSpec(memory_space=pl.ANY)
    cfg = (tp, nz, rows, tokens, half, hp, own_rows, d_model)
    blocks = pl.pallas_call(
        functools.partial(kernel, cfg),
        out_shape=jax.ShapeDtypeStruct((tp, 2 * rows, hd), BF16),
        in_specs=[vmem, vmem, vmem, vmem, vmem, hbm, vmem, vmem],
        out_specs=hbm,
        scratch_shapes=scratch,
        compiler_params=pltpu.CompilerParams(
            collective_id=0, has_side_effects=True, vmem_limit_bytes=62 * 1024 * 1024
        ),
        cost_estimate=pl.CostEstimate(
            flops=2 * tokens * own_rows * d_model,
            bytes_accessed=2 * own_rows * d_model,
            transcendentals=0,
        ),
    )(
        order, hidden, adapter_rows.reshape(1, own_rows), doubled, adapter_b,
        frozen_down_weight, residual, gain.astype(F32).reshape(2, hd),
    )
    return blocks.reshape(tp, 2, rows, hd).transpose(0, 2, 1, 3).reshape(tokens, d_model)


def solution(mesh):
    placed = (
        P("groups", "tp"),
        P("groups"),
        P("tp"),
        P("tp", None),
        P(None, "tp"),
        P("tp", None),
        P(("groups", "tp"), None),
        P(),
    )
    return jax.shard_map(
        on_device, mesh=mesh, in_specs=placed, out_specs=P("groups", None), check_vma=False
    )
```

```python
import functools

import jax
import jax.numpy as jnp
from jax import lax
from jax.experimental import pallas as pl
from jax.experimental.pallas import tpu as pltpu
from jax.sharding import PartitionSpec as P

adapter_scale = 2.0
norm_eps = 1e-05
CHUNKS = 8
PIECES = 4
W_SLOTS = 3
BF16 = jnp.bfloat16
F32 = jnp.float32
NT = (((1,), (1,)), ((), ()))


def kernel(
    cfg,
    pos_ref, hidden_ref, ids_ref, a_ref, b_ref, w_hbm, res_ref,
    out_hbm,
    wbuf, late, aa_ref, code, idrows, abuf, got, uacc, tsend, tcore, trecv, bfull,
    pbuf, c_send, c_recv, y_send, y_recv, y_own, z_send, z_recv, stream, nbuf,
    w_sem, cs, cr, ys, yr, zs, zr, as_, ar, ts, tr,
    bzs, bzr, bys, byr, bcs, bcr, bxs, bxr, axs, axr, tcs, tcr, gzs, gzr, gys, gyr, gcs, gcr, loc,
):
    tp, nz, rows, tokens, quarter, qp, held, own_rows, d_model = cfg
    n = CHUNKS
    hd = d_model // 2
    cw = hd // n
    me = lax.axis_index("tp")
    group = lax.axis_index("groups")
    side = group % 2
    z, y, c = me // 4, (me // 2) % 2, me % 2
    sib = me + 1 - 2 * c
    ypeer = me + 2 - 4 * y
    nb = 2 * nz

    def remote(src, dst, send, recv, dev):
        return pltpu.make_async_remote_copy(
            src_ref=src, dst_ref=dst, send_sem=send, recv_sem=recv,
            device_id={"tp": dev}, device_id_type=pl.DeviceIdType.MESH,
        )

    def across(src, dst, send, recv):
        return pltpu.make_async_remote_copy(
            src_ref=src, dst_ref=dst, send_sem=send, recv_sem=recv,
            device_id={"groups": group + 1 - 2 * side}, device_id_type=pl.DeviceIdType.MESH,
        )

    def w_copies(j):
        slot = lax.rem(j, W_SLOTS)
        return [
            pltpu.make_async_copy(
                w_hbm.at[:, pl.ds(pl.multiple_of(h * hd + j * cw, 128), cw)],
                wbuf.at[slot, :, pl.ds(h * cw, cw)],
                w_sem.at[slot, h],
            )
            for h in range(2)
        ]

    for j in range(W_SLOTS - 1):
        for copy in w_copies(j):
            copy.start()

    barrier = pltpu.get_barrier_semaphore()

    @pl.loop(1, tp)
    def _(i):
        pl.semaphore_signal(
            barrier, inc=1, device_id={"tp": lax.rem(me + i, tp)},
            device_id_type=pl.DeviceIdType.MESH,
        )

    pl.semaphore_signal(
        barrier, inc=1, device_id={"groups": group + 1 - 2 * side},
        device_id_type=pl.DeviceIdType.MESH,
    )

    buf_rows = hidden_ref.shape[0]
    wanted = pos_ref[...].reshape(1, tokens)
    pick = jnp.where(
        wanted == lax.broadcasted_iota(jnp.int32, (buf_rows, tokens), 0), 1.0, 0.0
    )
    pick = pick.T
    pick = jnp.concatenate(
        [
            pick[(4 * i + 2 * j + k) * rows : (4 * i + 2 * j + k + 1) * rows]
            for k in range(2) for j in range(2) for i in range(nz)
        ],
        axis=0,
    ).astype(BF16)
    lw = 256 if own_rows % 256 == 0 else 128
    for t in range(own_rows // lw):
        late[:, t * lw : (t + 1) * lw] = jnp.dot(
            pick, hidden_ref[:, t * lw : (t + 1) * lw], preferred_element_type=F32
        ).astype(BF16)

    uacc[...] = jnp.zeros_like(uacc)

    pl.semaphore_wait(barrier, tp)

    def find_slots():
        ids = ids_ref[...].reshape(1, own_rows)
        aa_ref[...] = jnp.concatenate([a_ref[...], a_ref[...]], axis=0)
        first = lax.broadcasted_iota(jnp.int32, (tp, 1), 0) * own_rows
        mine = (ids >= first) & (ids < first + own_rows)
        hot = jnp.where(mine, 1.0, 0.0)
        local = jnp.sum(jnp.where(mine, ids - first, 0), axis=0, keepdims=True)
        before = jnp.where(
            lax.broadcasted_iota(jnp.int32, (128, 128), 0)
            < lax.broadcasted_iota(jnp.int32, (128, 128), 1), 1.0, 0.0,
        ).astype(BF16)
        carry = jnp.zeros((tp, 1), F32) - (side * 2 * quarter).astype(F32)
        base = (lax.broadcasted_iota(jnp.int32, (tp, 1), 0) * 128).astype(F32)
        for t in range(own_rows // 128):
            part = hot[:, t * 128 : (t + 1) * 128]
            rank = jnp.dot(part.astype(BF16), before, preferred_element_type=F32) + carry
            spot = rank + base + jnp.where(rank >= quarter, 64.0 - quarter, 0.0)
            spot = jnp.where((rank >= 0.0) & (rank < 2.0 * quarter), spot, -1.0)
            code[:, t * 128 : (t + 1) * 128] = jnp.sum(
                part * spot, axis=0, keepdims=True
            ).astype(jnp.int32)
            carry = carry + jnp.sum(part, axis=1, keepdims=True)
        which = lax.broadcasted_iota(jnp.int32, (16, own_rows), 0)
        idrows[...] = jnp.where(
            which == 0, (local >> 7).astype(F32),
            jnp.where(which == 1, (local & 127).astype(F32), jnp.where(which == 2, 1.0, 0.0)),
        ).astype(BF16)

    def b_z(i):
        return remote(bfull.at[me, side], bfull.at[me, side], bzs.at[i - 1], bzr.at[i - 1], lax.rem(me + 4 * i, tp))

    def b_y(i):
        blk = lax.rem(me + 4 * nz - 4 * i, tp)
        return remote(bfull.at[blk, side], bfull.at[blk, side], bys.at[i], byr.at[i], ypeer)

    def b_c(i, other):
        blk = lax.rem(me + 4 * nz - 4 * i, tp)
        if other:
            blk = blk + 2 - 4 * y
        k = i + other * nz
        return remote(bfull.at[blk, side], bfull.at[blk, side], bcs.at[k], bcr.at[k], sib)

    def b_x():
        return across(bfull.at[:, side], bfull.at[:, side], bxs, bxr)

    br = b_ref.shape[0] // 2
    bfull[me, side] = b_ref[pl.ds(pl.multiple_of(side * br, 16), br), :]
    for i in range(1, nz):
        b_z(i).start()
    b_y(0).start()
    b_c(0, 0).start()

    def core_copy(j):
        return remote(c_send.at[j], c_recv.at[j], cs.at[j], cr.at[j], sib)

    def y_copy(j):
        return remote(y_send.at[j], y_recv.at[j], ys.at[j], yr.at[j], ypeer)

    def z_copy(j, i):
        to = lax.rem(z + i, nz)
        return remote(
            z_send.at[j, to], z_recv.at[j, i - 1], zs.at[j, i - 1], zr.at[j, i - 1],
            lax.rem(me + 4 * i, tp),
        )

    def a_copy(i):
        to = lax.rem(me + i, tp)
        return remote(abuf.at[to], got.at[i, side], as_.at[i], ar.at[i], to)

    def a_x(i):
        return across(got.at[i, side], got.at[i, side], axs.at[i], axr.at[i])

    def t_core():
        return remote(
            tsend.at[pl.ds((1 - c) * nb, nb)], tcore, tcs, tcr, sib
        )

    def t_copy(i):
        to = lax.rem(me + 2 * i, tp)
        blk = c * nb + ((to // 2) % 2) * nz + to // 4
        return remote(tsend.at[blk], trecv.at[i], ts.at[i], tr.at[i], to)

    lane = lax.broadcasted_iota(jnp.int32, (qp, 128), 1)
    per = 2 * tp // n

    def send_rows(i):
        to = lax.rem(me + i, tp)
        spot = jnp.where(
            code[...] == to * 128 + lax.broadcasted_iota(jnp.int32, (128, own_rows), 0), 1.0, 0.0
        ).astype(BF16)
        picked = lax.dot_general(spot, aa_ref[...], NT, preferred_element_type=F32)
        rows_out = jnp.where(lane < 64, picked[:qp], picked[64 : 64 + qp])
        marks = lax.dot_general(idrows[...], spot, NT, preferred_element_type=F32)
        parts = [rows_out, marks[:8]]
        if held > qp + 8:
            parts.append(jnp.zeros((held - qp - 8, 128), F32))
        block = jnp.concatenate(parts, axis=0).astype(BF16)

        @pl.when(i > 0)
        def _():
            abuf[to] = block
            a_copy(i).start()

        @pl.when(i == 0)
        def _():
            got[0, side] = block

    def pass_rows(i):
        @pl.when(i > 0)
        def _():
            a_copy(i).wait_recv()

        a_x(i).start()

    def use_rows(i):
        a_x(i).wait_recv()
        block = got[i].reshape(2 * held, 128)
        found = []
        for h in range(2):
            m = block[h * held + qp : h * held + qp + 8].astype(F32)
            found.append(
                jnp.where(m[2:3] > 0.5, m[0:1] * 128.0 + m[1:2], -1.0).astype(jnp.int32)
            )
        row = jnp.concatenate(
            [found[0][:, :64], found[1][:, :64], found[0][:, 64:], found[1][:, 64:]], axis=1
        )
        spot = jnp.where(
            row == lax.broadcasted_iota(jnp.int32, (own_rows, 256), 0), 1.0, 0.0
        ).astype(BF16)
        lq = jnp.dot(late[...], spot, preferred_element_type=F32).astype(BF16)
        for q in range(2):
            part = lq[:, 128 * q : 128 * q + 128]
            if held < 64:
                part = jnp.concatenate([part[:, :held], part[:, 64 : 64 + held]], axis=1)
            uacc[q] += jnp.dot(part, block, preferred_element_type=F32)

    @pl.loop(0, n + 5)
    def _(s):
        @pl.when(s < n)
        def _():
            @pl.when(s + W_SLOTS - 1 < n)
            def _():
                for copy in w_copies(s + W_SLOTS - 1):
                    copy.start()

            for copy in w_copies(s):
                copy.wait()
            slot, ps = lax.rem(s, W_SLOTS), lax.rem(s, 2)
            for h in range(2):
                r = jnp.dot(
                    late[...], wbuf[slot, :, h * cw : (h + 1) * cw], preferred_element_type=F32
                )
                pbuf[ps, :, h * rows : (h + 1) * rows, :] = r.reshape(tp, rows, cw)
            c_send[s] = pbuf[ps, pl.ds((1 - c) * nb, nb)].astype(BF16)
            core_copy(s).start()

        @pl.when((s >= 1) & (s < n + 1))
        def _():
            j = s - 1
            ps = lax.rem(j, 2)
            core_copy(j).wait_recv()
            y_send[j] = (
                pbuf[ps, pl.ds(c * nb + (1 - y) * nz, nz)]
                + c_recv[j, pl.ds((1 - y) * nz, nz)].astype(F32)
            ).astype(BF16)
            y_copy(j).start()
            y_own[j] = pbuf[ps, pl.ds(c * nb + y * nz, nz)] + c_recv[
                j, pl.ds(y * nz, nz)
            ].astype(F32)

        @pl.when(s == 0)
        def _():
            find_slots()

        @pl.when(s < n // 2)
        def _():
            @pl.loop(0, per)
            def _(k):
                send_rows(s * per + k)

        @pl.when((s >= 2) & (s < n // 2 + 2))
        def _():
            @pl.loop(0, per)
            def _(k):
                pass_rows((s - 2) * per + k)

        @pl.when((s >= n // 2) & (s < n))
        def _():
            @pl.loop(0, per)
            def _(k):
                use_rows((s - n // 2) * per + k)

        @pl.when(s == 1)
        def _():
            for i in range(1, nz):
                b_z(i).wait_recv()
                b_y(i).start()
                b_c(i, 0).start()

        @pl.when(s == 3)
        def _():
            for i in range(nz):
                b_y(i).wait_recv()
                b_c(i, 1).start()

        @pl.when(s == 5)
        def _():
            for i in range(nz):
                b_c(i, 0).wait_recv()
                b_c(i, 1).wait_recv()
            b_x().start()

        @pl.when(s == n - 1)
        def _():
            low = uacc[0][:, :64] + uacc[1][:, 64:]
            low = jnp.concatenate([low, jnp.zeros_like(low)], axis=1)
            tsend[...] = low.reshape(tp, rows, 128)

            t_core().start()

        @pl.when(s == n)
        def _():
            t_core().wait()
            tsend[pl.ds(c * nb, nb)] = tsend[pl.ds(c * nb, nb)] + tcore[...]

            @pl.loop(1, tp // 2)
            def _(i):
                t_copy(i).start()

        @pl.when((s >= 3) & (s < n + 3))
        def _():
            j = s - 3
            y_copy(j).wait_recv()
            total = y_own[j] + y_recv[j].astype(F32)
            z_send[j] = total.astype(BF16)
            for i in range(1, nz):
                z_copy(j, i).start()
            y_own[j] = total

        @pl.when(s >= 5)
        def _():
            j = s - 5
            total = y_own[j, z]
            for i in range(1, nz):
                z_copy(j, i).wait_recv()
                total = total + z_recv[j, i - 1].astype(F32)
            stream[:, pl.ds(pl.multiple_of(j * cw, 128), cw)] = total

    @pl.loop(1, tp // 2)
    def _(i):
        t_copy(i).wait_recv()

    low = tsend[c * nb + y * nz + z]
    for i in range(1, tp // 2):
        low = low + trecv[i]
    low = (low[:, :64] * adapter_scale).astype(BF16)
    b_x().wait_recv()
    bw = d_model // tp
    square = jnp.zeros((rows, 1), F32)
    for k in range(tp):
        h, at = (k * bw) // hd, (k * bw) % hd
        v = stream[h * rows : (h + 1) * rows, at : at + bw]
        v = v + res_ref[:, k * bw : (k + 1) * bw].astype(F32)
        v = v + jnp.dot(low, bfull[k].reshape(2 * br, bw), preferred_element_type=F32)
        stream[h * rows : (h + 1) * rows, at : at + bw] = v
        square = square + jnp.sum(v * v, axis=1, keepdims=True)
    inverse = lax.rsqrt(square * (1.0 / d_model) + norm_eps)

    pw = d_model // PIECES

    def piece(ref, p):
        return ref.at[:, pl.ds(p * pw, pw)]

    def g_own(p):
        return pltpu.make_async_copy(piece(nbuf, p), piece(out_hbm.at[me], p), loc.at[p])

    def g_z(p, i):
        return remote(
            piece(nbuf, p), piece(out_hbm.at[me], p), gzs.at[p, i - 1], gzr.at[p, i - 1],
            lax.rem(me + 4 * i, tp),
        )

    def g_blk(i):
        return lax.rem(me + 4 * nz - 4 * i, tp)

    def g_y(p, i):
        dst = piece(out_hbm.at[g_blk(i)], p)
        src = piece(nbuf, p) if i == 0 else dst
        return remote(src, dst, gys.at[p, i], gyr.at[p, i], ypeer)

    def g_c(p, i, other):
        blk = g_blk(i) + (2 - 4 * y if other else 0)
        dst = piece(out_hbm.at[blk], p)
        src = piece(nbuf, p) if (i == 0 and not other) else dst
        k = i + other * nz
        return remote(src, dst, gcs.at[p, k], gcr.at[p, k], sib)

    for p in range(PIECES):
        h, at = (p * pw) // hd, (p * pw) % hd
        nbuf[:, p * pw : (p + 1) * pw] = (
            stream[h * rows : (h + 1) * rows, at : at + pw] * inverse
        ).astype(BF16)
        g_y(p, 0).start()
        for i in range(1, nz):
            g_z(p, i).start()
        g_c(p, 0, 0).start()
        g_own(p).start()

    items = [(p, i) for p in range(PIECES) for i in range(nz)]
    lag = nz
    for q in range(len(items) + lag):
        if q < len(items):
            p, i = items[q]
            if i > 0:
                g_z(p, i).wait_recv()
                g_y(p, i).start()
                g_c(p, i, 0).start()
        if q >= lag:
            p, i = items[q - lag]
            g_y(p, i).wait_recv()
            g_c(p, i, 1).start()

    for p in range(PIECES):
        g_own(p).wait()
        for i in range(nz):
            g_c(p, i, 0).wait()
            g_c(p, i, 1).wait()
            g_y(p, i).wait_send()
            if i > 0:
                g_z(p, i).wait_send()
    for i in range(nz):
        b_y(i).wait_send()
        b_c(i, 0).wait_send()
        b_c(i, 1).wait_send()
        if i > 0:
            b_z(i).wait_send()

    @pl.loop(1, tp)
    def _(i):
        a_copy(i).wait_send()

    @pl.loop(1, tp // 2)
    def _(i):
        t_copy(i).wait_send()

    @pl.loop(0, tp)
    def _(i):
        a_x(i).wait_send()

    b_x().wait_send()

    @pl.loop(0, n)
    def _(j):
        core_copy(j).wait_send()
        y_copy(j).wait_send()
        for i in range(1, nz):
            z_copy(j, i).wait_send()


def on_device(
    hidden, positions, adapter_rows, adapter_a, adapter_b, frozen_down_weight, residual, gain
):
    tp = lax.axis_size("tp")
    nz = tp // 4
    rows, d_model = residual.shape
    own_rows = frozen_down_weight.shape[0]
    tokens = rows * tp
    quarter = -(-2 * own_rows // tp // 4)
    qp = (quarter + 7) // 8 * 8
    held = (qp + 8 + 15) // 16 * 16
    hd = d_model // 2
    cw = hd // CHUNKS
    n = CHUNKS
    dma = pltpu.SemaphoreType.DMA
    blk = (2 * rows, cw)
    scratch = [
        pltpu.VMEM((W_SLOTS, own_rows, 2 * cw), BF16),
        pltpu.VMEM((tokens, own_rows), BF16),
        pltpu.VMEM((128, own_rows), BF16),
        pltpu.VMEM((1, own_rows), jnp.int32),
        pltpu.VMEM((16, own_rows), BF16),
        pltpu.VMEM((tp, held, 128), BF16),
        pltpu.VMEM((tp, 2, held, 128), BF16),
        pltpu.VMEM((2, tokens, 128), F32),
        pltpu.VMEM((tp, rows, 128), F32),
        pltpu.VMEM((tp // 2, rows, 128), F32),
        pltpu.VMEM((tp // 2, rows, 128), F32),
        pltpu.VMEM((tp, 2, adapter_b.shape[0] // 2, adapter_b.shape[1]), BF16),
        pltpu.VMEM((2, tp) + blk, F32),
        pltpu.VMEM((n, 2 * nz) + blk, BF16),
        pltpu.VMEM((n, 2 * nz) + blk, BF16),
        pltpu.VMEM((n, nz) + blk, BF16),
        pltpu.VMEM((n, nz) + blk, BF16),
        pltpu.VMEM((n, nz) + blk, F32),
        pltpu.VMEM((n, nz) + blk, BF16),
        pltpu.VMEM((n, nz - 1) + blk, BF16),
        pltpu.VMEM((2 * rows, hd), F32),
        pltpu.VMEM((rows, d_model), BF16),
        dma((W_SLOTS, 2)),
        dma((n,)), dma((n,)),
        dma((n,)), dma((n,)),
        dma((n, nz - 1)), dma((n, nz - 1)),
        dma((tp,)), dma((tp,)),
        dma((tp,)), dma((tp,)),
        dma((nz - 1,)), dma((nz - 1,)),
        dma((nz,)), dma((nz,)),
        dma((2 * nz,)), dma((2 * nz,)),
        dma, dma, dma((tp,)), dma((tp,)), dma, dma,
        dma((PIECES, nz - 1)), dma((PIECES, nz - 1)),
        dma((PIECES, nz)), dma((PIECES, nz)),
        dma((PIECES, 2 * nz)), dma((PIECES, 2 * nz)),
        dma((PIECES,)),
    ]
    vmem = pl.BlockSpec(memory_space=pltpu.VMEM)
    small = 2 * tokens * d_model <= 8 * 1024 * 1024
    shape = (tp, rows, d_model)
    hbm = pl.BlockSpec(memory_space=pl.ANY)
    cfg = (tp, nz, rows, tokens, quarter, qp, held, own_rows, d_model)
    blocks = pl.pallas_call(
        functools.partial(kernel, cfg),
        out_shape=pltpu.VMEM(shape, BF16) if small else jax.ShapeDtypeStruct(shape, BF16),
        in_specs=[vmem, vmem, vmem, vmem, vmem, hbm, vmem],
        out_specs=vmem if small else hbm,
        scratch_shapes=scratch,
        compiler_params=pltpu.CompilerParams(
            collective_id=0, has_side_effects=True, vmem_limit_bytes=(52 if small else 62) * 1024 * 1024
        ),
        cost_estimate=pl.CostEstimate(
            flops=2 * tokens * own_rows * d_model,
            bytes_accessed=2 * own_rows * d_model,
            transcendentals=0,
        ),
    )(
        positions, hidden, adapter_rows, adapter_a.T, adapter_b, frozen_down_weight, residual,
    )
    scaled = blocks.reshape(tokens, d_model).astype(F32) * gain.astype(F32)
    return scaled.astype(BF16)


def solution(mesh):
    placed = (
        P("groups", "tp"),
        P("groups"),
        P("tp"),
        P("tp", None),
        P(None, "tp"),
        P("tp", None),
        P(("groups", "tp"), None),
        P(),
    )
    return jax.shard_map(
        on_device, mesh=mesh, in_specs=placed, out_specs=P("groups", None), check_vma=False
    )
```

```python
import functools

import jax
import jax.numpy as jnp
from jax import lax
from jax.experimental import pallas as pl
from jax.experimental.pallas import tpu as pltpu
from jax.sharding import PartitionSpec as P

adapter_scale = 2.0
norm_eps = 1e-05
CHUNKS = 8
PIECES = 4
W_SLOTS = 3
BF16 = jnp.bfloat16
F32 = jnp.float32
NT = (((1,), (1,)), ((), ()))


def kernel(
    cfg,
    pos_ref, hidden_ref, ids_ref, a_ref, b_ref, w_hbm, res_ref,
    out_hbm,
    wbuf, late, aa_ref, code, idrows, abuf, got, uacc, tsend, tcore, trecv, bfull,
    pbuf, c_send, c_recv, y_send, y_recv, y_own, z_send, z_recv, stream, nbuf,
    w_sem, cs, cr, ys, yr, zs, zr, as_, ar, ts, tr,
    bzs, bzr, bys, byr, bcs, bcr, bxs, bxr, axs, axr, tcs, tcr, gzs, gzr, gys, gyr, gcs, gcr, loc,
):
    tp, nz, rows, tokens, quarter, qp, held, own_rows, d_model = cfg
    n = CHUNKS
    hd = d_model // 2
    cw = hd // n
    me = lax.axis_index("tp")
    group = lax.axis_index("groups")
    side = group % 2
    z, y, c = me // 4, (me // 2) % 2, me % 2
    sib = me + 1 - 2 * c
    ypeer = me + 2 - 4 * y
    nb = 2 * nz

    def remote(src, dst, send, recv, dev):
        return pltpu.make_async_remote_copy(
            src_ref=src, dst_ref=dst, send_sem=send, recv_sem=recv,
            device_id={"tp": dev}, device_id_type=pl.DeviceIdType.MESH,
        )

    def across(src, dst, send, recv):
        return pltpu.make_async_remote_copy(
            src_ref=src, dst_ref=dst, send_sem=send, recv_sem=recv,
            device_id={"groups": group + 1 - 2 * side}, device_id_type=pl.DeviceIdType.MESH,
        )

    def w_copies(j):
        slot = lax.rem(j, W_SLOTS)
        return [
            pltpu.make_async_copy(
                w_hbm.at[:, pl.ds(pl.multiple_of(h * hd + j * cw, 128), cw)],
                wbuf.at[slot, :, pl.ds(h * cw, cw)],
                w_sem.at[slot, h],
            )
            for h in range(2)
        ]

    for j in range(W_SLOTS - 1):
        for copy in w_copies(j):
            copy.start()

    barrier = pltpu.get_barrier_semaphore()

    @pl.loop(1, tp)
    def _(i):
        pl.semaphore_signal(
            barrier, inc=1, device_id={"tp": lax.rem(me + i, tp)},
            device_id_type=pl.DeviceIdType.MESH,
        )

    pl.semaphore_signal(
        barrier, inc=1, device_id={"groups": group + 1 - 2 * side},
        device_id_type=pl.DeviceIdType.MESH,
    )

    buf_rows = hidden_ref.shape[0]
    wanted = pos_ref[...].reshape(1, tokens)
    pick = jnp.where(
        wanted == lax.broadcasted_iota(jnp.int32, (buf_rows, tokens), 0), 1.0, 0.0
    )
    pick = pick.T
    pick = jnp.concatenate(
        [
            pick[(4 * i + 2 * j + k) * rows : (4 * i + 2 * j + k + 1) * rows]
            for k in range(2) for j in range(2) for i in range(nz)
        ],
        axis=0,
    ).astype(BF16)
    lw = 256 if own_rows % 256 == 0 else 128
    for t in range(own_rows // lw):
        late[:, t * lw : (t + 1) * lw] = jnp.dot(
            pick, hidden_ref[:, t * lw : (t + 1) * lw], preferred_element_type=F32
        ).astype(BF16)

    uacc[...] = jnp.zeros_like(uacc)

    pl.semaphore_wait(barrier, tp)

    def find_slots():
        ids = ids_ref[...].reshape(1, own_rows)
        aa_ref[...] = jnp.concatenate([a_ref[...], a_ref[...]], axis=0)
        first = lax.broadcasted_iota(jnp.int32, (tp, 1), 0) * own_rows
        mine = (ids >= first) & (ids < first + own_rows)
        hot = jnp.where(mine, 1.0, 0.0)
        local = jnp.sum(jnp.where(mine, ids - first, 0), axis=0, keepdims=True)
        before = jnp.where(
            lax.broadcasted_iota(jnp.int32, (128, 128), 0)
            < lax.broadcasted_iota(jnp.int32, (128, 128), 1), 1.0, 0.0,
        ).astype(BF16)
        carry = jnp.zeros((tp, 1), F32) - (side * 2 * quarter).astype(F32)
        base = (lax.broadcasted_iota(jnp.int32, (tp, 1), 0) * 128).astype(F32)
        for t in range(own_rows // 128):
            part = hot[:, t * 128 : (t + 1) * 128]
            rank = jnp.dot(part.astype(BF16), before, preferred_element_type=F32) + carry
            spot = rank + base + jnp.where(rank >= quarter, 64.0 - quarter, 0.0)
            spot = jnp.where((rank >= 0.0) & (rank < 2.0 * quarter), spot, -1.0)
            code[:, t * 128 : (t + 1) * 128] = jnp.sum(
                part * spot, axis=0, keepdims=True
            ).astype(jnp.int32)
            carry = carry + jnp.sum(part, axis=1, keepdims=True)
        which = lax.broadcasted_iota(jnp.int32, (16, own_rows), 0)
        idrows[...] = jnp.where(
            which == 0, (local >> 7).astype(F32),
            jnp.where(which == 1, (local & 127).astype(F32), jnp.where(which == 2, 1.0, 0.0)),
        ).astype(BF16)

    def b_z(i):
        return remote(bfull.at[me, side], bfull.at[me, side], bzs.at[i - 1], bzr.at[i - 1], lax.rem(me + 4 * i, tp))

    def b_y(i):
        blk = lax.rem(me + 4 * nz - 4 * i, tp)
        return remote(bfull.at[blk, side], bfull.at[blk, side], bys.at[i], byr.at[i], ypeer)

    def b_c(i, other):
        blk = lax.rem(me + 4 * nz - 4 * i, tp)
        if other:
            blk = blk + 2 - 4 * y
        k = i + other * nz
        return remote(bfull.at[blk, side], bfull.at[blk, side], bcs.at[k], bcr.at[k], sib)

    def b_x():
        return across(bfull.at[:, side], bfull.at[:, side], bxs, bxr)

    br = b_ref.shape[0] // 2
    bfull[me, side] = b_ref[pl.ds(pl.multiple_of(side * br, 16), br), :]
    for i in range(1, nz):
        b_z(i).start()
    b_y(0).start()
    b_c(0, 0).start()

    def core_copy(j):
        return remote(c_send.at[j], c_recv.at[j], cs.at[j], cr.at[j], sib)

    def y_copy(j):
        return remote(y_send.at[j], y_recv.at[j], ys.at[j], yr.at[j], ypeer)

    def z_copy(j, i):
        to = lax.rem(z + i, nz)
        return remote(
            z_send.at[j, to], z_recv.at[j, i - 1], zs.at[j, i - 1], zr.at[j, i - 1],
            lax.rem(me + 4 * i, tp),
        )

    def a_copy(i):
        to = lax.rem(me + i, tp)
        return remote(abuf.at[to], got.at[i, side], as_.at[i], ar.at[i], to)

    def a_x(i):
        return across(got.at[i, side], got.at[i, side], axs.at[i], axr.at[i])

    def t_core():
        return remote(
            tsend.at[pl.ds((1 - c) * nb, nb)], tcore, tcs, tcr, sib
        )

    def t_copy(i):
        to = lax.rem(me + 2 * i, tp)
        blk = c * nb + ((to // 2) % 2) * nz + to // 4
        return remote(tsend.at[blk], trecv.at[i], ts.at[i], tr.at[i], to)

    lane = lax.broadcasted_iota(jnp.int32, (qp, 128), 1)
    per = tp // n

    def send_rows(i):
        to = lax.rem(me + i, tp)
        spot = jnp.where(
            code[...] == to * 128 + lax.broadcasted_iota(jnp.int32, (128, own_rows), 0), 1.0, 0.0
        ).astype(BF16)
        picked = lax.dot_general(spot, aa_ref[...], NT, preferred_element_type=F32)
        rows_out = jnp.where(lane < 64, picked[:qp], picked[64 : 64 + qp])
        marks = lax.dot_general(idrows[...], spot, NT, preferred_element_type=F32)
        parts = [rows_out, marks[:8]]
        if held > qp + 8:
            parts.append(jnp.zeros((held - qp - 8, 128), F32))
        block = jnp.concatenate(parts, axis=0).astype(BF16)

        @pl.when(i > 0)
        def _():
            abuf[to] = block
            a_copy(i).start()

        @pl.when(i == 0)
        def _():
            got[0, side] = block

    def pass_rows(i):
        @pl.when(i > 0)
        def _():
            a_copy(i).wait_recv()

        a_x(i).start()

    def use_rows(i):
        a_x(i).wait_recv()
        block = got[i].reshape(2 * held, 128)
        found = []
        for h in range(2):
            m = block[h * held + qp : h * held + qp + 8].astype(F32)
            found.append(
                jnp.where(m[2:3] > 0.5, m[0:1] * 128.0 + m[1:2], -1.0).astype(jnp.int32)
            )
        row = jnp.concatenate(
            [found[0][:, :64], found[1][:, :64], found[0][:, 64:], found[1][:, 64:]], axis=1
        )
        spot = jnp.where(
            row == lax.broadcasted_iota(jnp.int32, (own_rows, 256), 0), 1.0, 0.0
        ).astype(BF16)
        lq = jnp.dot(late[...], spot, preferred_element_type=F32).astype(BF16)
        for q in range(2):
            part = lq[:, 128 * q : 128 * q + 128]
            if held < 64:
                part = jnp.concatenate([part[:, :held], part[:, 64 : 64 + held]], axis=1)
            uacc[q] += jnp.dot(part, block, preferred_element_type=F32)

    @pl.loop(0, n + 5)
    def _(s):
        @pl.when(s < n)
        def _():
            @pl.when(s + W_SLOTS - 1 < n)
            def _():
                for copy in w_copies(s + W_SLOTS - 1):
                    copy.start()

            for copy in w_copies(s):
                copy.wait()
            slot, ps = lax.rem(s, W_SLOTS), lax.rem(s, 2)
            for h in range(2):
                r = jnp.dot(
                    late[...], wbuf[slot, :, h * cw : (h + 1) * cw], preferred_element_type=F32
                )
                pbuf[ps, :, h * rows : (h + 1) * rows, :] = r.reshape(tp, rows, cw)
            c_send[s] = pbuf[ps, pl.ds((1 - c) * nb, nb)].astype(BF16)
            core_copy(s).start()

        @pl.when((s >= 1) & (s < n + 1))
        def _():
            j = s - 1
            ps = lax.rem(j, 2)
            core_copy(j).wait_recv()
            y_send[j] = (
                pbuf[ps, pl.ds(c * nb + (1 - y) * nz, nz)]
                + c_recv[j, pl.ds((1 - y) * nz, nz)].astype(F32)
            ).astype(BF16)
            y_copy(j).start()
            y_own[j] = pbuf[ps, pl.ds(c * nb + y * nz, nz)] + c_recv[
                j, pl.ds(y * nz, nz)
            ].astype(F32)

        @pl.when(s == 0)
        def _():
            find_slots()

        @pl.when(s < n)
        def _():
            @pl.loop(0, per)
            def _(k):
                send_rows(s * per + k)

        @pl.when((s >= 2) & (s < n + 2))
        def _():
            @pl.loop(0, per)
            def _(k):
                pass_rows((s - 2) * per + k)

        @pl.when(s == 1)
        def _():
            for i in range(1, nz):
                b_z(i).wait_recv()
                b_y(i).start()
                b_c(i, 0).start()

        @pl.when(s == 3)
        def _():
            for i in range(nz):
                b_y(i).wait_recv()
                b_c(i, 1).start()

        @pl.when(s == 5)
        def _():
            for i in range(nz):
                b_c(i, 0).wait_recv()
                b_c(i, 1).wait_recv()
            b_x().start()

        @pl.when(s == n + 3)
        def _():
            t_core().wait()
            tsend[pl.ds(c * nb, nb)] = tsend[pl.ds(c * nb, nb)] + tcore[...]

            @pl.loop(1, tp // 2)
            def _(i):
                t_copy(i).start()

        @pl.when((s >= 3) & (s < n + 3))
        def _():
            j = s - 3
            y_copy(j).wait_recv()
            total = y_own[j] + y_recv[j].astype(F32)
            z_send[j] = total.astype(BF16)
            for i in range(1, nz):
                z_copy(j, i).start()
            y_own[j] = total

        @pl.when(s >= 5)
        def _():
            j = s - 5
            total = y_own[j, z]
            for i in range(1, nz):
                z_copy(j, i).wait_recv()
                total = total + z_recv[j, i - 1].astype(F32)
            stream[:, pl.ds(pl.multiple_of(j * cw, 128), cw)] = total

        @pl.when((s >= n - 1) & (s < n + 3))
        def _():
            @pl.loop(0, 2 * per)
            def _(k):
                use_rows((s - n + 1) * 2 * per + k)

        @pl.when(s == n + 2)
        def _():
            low = uacc[0][:, :64] + uacc[1][:, 64:]
            low = jnp.concatenate([low, jnp.zeros_like(low)], axis=1)
            tsend[...] = low.reshape(tp, rows, 128)

            t_core().start()

    @pl.loop(1, tp // 2)
    def _(i):
        t_copy(i).wait_recv()

    low = tsend[c * nb + y * nz + z]
    for i in range(1, tp // 2):
        low = low + trecv[i]
    low = (low[:, :64] * adapter_scale).astype(BF16)
    b_x().wait_recv()
    bw = d_model // tp
    square = jnp.zeros((rows, 1), F32)
    for k in range(tp):
        h, at = (k * bw) // hd, (k * bw) % hd
        v = stream[h * rows : (h + 1) * rows, at : at + bw]
        v = v + res_ref[:, k * bw : (k + 1) * bw].astype(F32)
        v = v + jnp.dot(low, bfull[k].reshape(2 * br, bw), preferred_element_type=F32)
        stream[h * rows : (h + 1) * rows, at : at + bw] = v
        square = square + jnp.sum(v * v, axis=1, keepdims=True)
    inverse = lax.rsqrt(square * (1.0 / d_model) + norm_eps)

    pw = d_model // PIECES

    def piece(ref, p):
        return ref.at[:, pl.ds(p * pw, pw)]

    def g_own(p):
        return pltpu.make_async_copy(piece(nbuf, p), piece(out_hbm.at[me], p), loc.at[p])

    def g_z(p, i):
        return remote(
            piece(nbuf, p), piece(out_hbm.at[me], p), gzs.at[p, i - 1], gzr.at[p, i - 1],
            lax.rem(me + 4 * i, tp),
        )

    def g_blk(i):
        return lax.rem(me + 4 * nz - 4 * i, tp)

    def g_y(p, i):
        dst = piece(out_hbm.at[g_blk(i)], p)
        src = piece(nbuf, p) if i == 0 else dst
        return remote(src, dst, gys.at[p, i], gyr.at[p, i], ypeer)

    def g_c(p, i, other):
        blk = g_blk(i) + (2 - 4 * y if other else 0)
        dst = piece(out_hbm.at[blk], p)
        src = piece(nbuf, p) if (i == 0 and not other) else dst
        k = i + other * nz
        return remote(src, dst, gcs.at[p, k], gcr.at[p, k], sib)

    for p in range(PIECES):
        h, at = (p * pw) // hd, (p * pw) % hd
        nbuf[:, p * pw : (p + 1) * pw] = (
            stream[h * rows : (h + 1) * rows, at : at + pw] * inverse
        ).astype(BF16)
        g_y(p, 0).start()
        for i in range(1, nz):
            g_z(p, i).start()
        g_c(p, 0, 0).start()
        g_own(p).start()

    items = [(p, i) for p in range(PIECES) for i in range(nz)]
    lag = nz
    for q in range(len(items) + lag):
        if q < len(items):
            p, i = items[q]
            if i > 0:
                g_z(p, i).wait_recv()
                g_y(p, i).start()
                g_c(p, i, 0).start()
        if q >= lag:
            p, i = items[q - lag]
            g_y(p, i).wait_recv()
            g_c(p, i, 1).start()

    for p in range(PIECES):
        g_own(p).wait()
        for i in range(nz):
            g_c(p, i, 0).wait()
            g_c(p, i, 1).wait()
            g_y(p, i).wait_send()
            if i > 0:
                g_z(p, i).wait_send()
    for i in range(nz):
        b_y(i).wait_send()
        b_c(i, 0).wait_send()
        b_c(i, 1).wait_send()
        if i > 0:
            b_z(i).wait_send()

    @pl.loop(1, tp)
    def _(i):
        a_copy(i).wait_send()

    @pl.loop(1, tp // 2)
    def _(i):
        t_copy(i).wait_send()

    @pl.loop(0, tp)
    def _(i):
        a_x(i).wait_send()

    b_x().wait_send()

    @pl.loop(0, n)
    def _(j):
        core_copy(j).wait_send()
        y_copy(j).wait_send()
        for i in range(1, nz):
            z_copy(j, i).wait_send()


def on_device(
    hidden, positions, adapter_rows, adapter_a, adapter_b, frozen_down_weight, residual, gain
):
    tp = lax.axis_size("tp")
    nz = tp // 4
    rows, d_model = residual.shape
    own_rows = frozen_down_weight.shape[0]
    tokens = rows * tp
    quarter = -(-2 * own_rows // tp // 4)
    qp = (quarter + 7) // 8 * 8
    held = (qp + 8 + 15) // 16 * 16
    hd = d_model // 2
    cw = hd // CHUNKS
    n = CHUNKS
    dma = pltpu.SemaphoreType.DMA
    blk = (2 * rows, cw)
    scratch = [
        pltpu.VMEM((W_SLOTS, own_rows, 2 * cw), BF16),
        pltpu.VMEM((tokens, own_rows), BF16),
        pltpu.VMEM((128, own_rows), BF16),
        pltpu.VMEM((1, own_rows), jnp.int32),
        pltpu.VMEM((16, own_rows), BF16),
        pltpu.VMEM((tp, held, 128), BF16),
        pltpu.VMEM((tp, 2, held, 128), BF16),
        pltpu.VMEM((2, tokens, 128), F32),
        pltpu.VMEM((tp, rows, 128), F32),
        pltpu.VMEM((tp // 2, rows, 128), F32),
        pltpu.VMEM((tp // 2, rows, 128), F32),
        pltpu.VMEM((tp, 2, adapter_b.shape[0] // 2, adapter_b.shape[1]), BF16),
        pltpu.VMEM((2, tp) + blk, F32),
        pltpu.VMEM((n, 2 * nz) + blk, BF16),
        pltpu.VMEM((n, 2 * nz) + blk, BF16),
        pltpu.VMEM((n, nz) + blk, BF16),
        pltpu.VMEM((n, nz) + blk, BF16),
        pltpu.VMEM((n, nz) + blk, F32),
        pltpu.VMEM((n, nz) + blk, BF16),
        pltpu.VMEM((n, nz - 1) + blk, BF16),
        pltpu.VMEM((2 * rows, hd), F32),
        pltpu.VMEM((rows, d_model), BF16),
        dma((W_SLOTS, 2)),
        dma((n,)), dma((n,)),
        dma((n,)), dma((n,)),
        dma((n, nz - 1)), dma((n, nz - 1)),
        dma((tp,)), dma((tp,)),
        dma((tp,)), dma((tp,)),
        dma((nz - 1,)), dma((nz - 1,)),
        dma((nz,)), dma((nz,)),
        dma((2 * nz,)), dma((2 * nz,)),
        dma, dma, dma((tp,)), dma((tp,)), dma, dma,
        dma((PIECES, nz - 1)), dma((PIECES, nz - 1)),
        dma((PIECES, nz)), dma((PIECES, nz)),
        dma((PIECES, 2 * nz)), dma((PIECES, 2 * nz)),
        dma((PIECES,)),
    ]
    vmem = pl.BlockSpec(memory_space=pltpu.VMEM)
    small = 2 * tokens * d_model <= 8 * 1024 * 1024
    shape = (tp, rows, d_model)
    hbm = pl.BlockSpec(memory_space=pl.ANY)
    cfg = (tp, nz, rows, tokens, quarter, qp, held, own_rows, d_model)
    blocks = pl.pallas_call(
        functools.partial(kernel, cfg),
        out_shape=pltpu.VMEM(shape, BF16) if small else jax.ShapeDtypeStruct(shape, BF16),
        in_specs=[vmem, vmem, vmem, vmem, vmem, hbm, vmem],
        out_specs=vmem if small else hbm,
        scratch_shapes=scratch,
        compiler_params=pltpu.CompilerParams(
            collective_id=0, has_side_effects=True, vmem_limit_bytes=(52 if small else 62) * 1024 * 1024
        ),
        cost_estimate=pl.CostEstimate(
            flops=2 * tokens * own_rows * d_model,
            bytes_accessed=2 * own_rows * d_model,
            transcendentals=0,
        ),
    )(
        positions, hidden, adapter_rows, adapter_a.T, adapter_b, frozen_down_weight, residual,
    )
    scaled = blocks.reshape(tokens, d_model).astype(F32) * gain.astype(F32)
    return scaled.astype(BF16)


def solution(mesh):
    placed = (
        P("groups", "tp"),
        P("groups"),
        P("tp"),
        P("tp", None),
        P(None, "tp"),
        P("tp", None),
        P(("groups", "tp"), None),
        P(),
    )
    return jax.shard_map(
        on_device, mesh=mesh, in_specs=placed, out_specs=P("groups", None), check_vma=False
    )
```
